512 devices in a mesh: ops: 32 (over y, x), sec: 16 (over z, core).
Axes of the slice: x: 4, y: 8, z: 8, core: 2. Of those that a mesh axis runs over, the one named last changes fastest.
Arguments:
- wavefunction: bfloat16 [32, 256, 256], P('sec'), may hold values from -6 to 6
- left_ops: bfloat16 [256, 32, 256, 256], P('ops', 'sec')
- right_ops: bfloat16 [256, 32, 256, 256], P('ops', 'sec')
- charge: int32 [256], P('ops'), may hold values from 0 to 31
- block_sizes: int32 [32], replicated, may hold values from 64 to 256, as said below
Outputs:
- sigma: bfloat16 [32, 256, 256], P('sec', 'ops')
- residual: bfloat16 [32, 256, 256], P('sec', 'ops')
The draws below stay inside these ranges and needn't reach their ends.
Inputs may be any that keep to these rules, and one draw needn't show every extreme that they name: `block_sizes`: every sector's live size lies between 64 and 256; rows and columns at or past it are padding; at least one sector is full.
All inputs are finite; a program needn't handle non-finite values.
Results may differ from the reference program's by a relative error of at most 0.005.
Values may be sent and summed in bfloat16 or wider, within the bound.
No kernel may reach another device: no remote copies, remote signals or barrier semaphores. Data moves between devices by JAX's collectives and lax.ppermute only.
A program may use at most 64 MiB of HBM per device.

```python
import jax
import jax.numpy as jnp
from jax import lax

BLOCK = 256
SECTORS = 32
PAIRS = 256


def build_blocks(noise, key_gain, key_rough):
    gains = jax.random.uniform(key_gain, (PAIRS, SECTORS, 1), jnp.float32, -1.5, 1.5)
    rough = jax.random.uniform(key_rough, (PAIRS, SECTORS, BLOCK), jnp.float32, 0.5, 1.5)
    diagonal = gains * rough
    row_of_indices = jnp.arange(BLOCK, dtype=jnp.int32)
    identity = (row_of_indices[:, None] == row_of_indices[None, :]).astype(jnp.float32)
    blocks = noise * (0.5 / BLOCK ** 0.5) + identity * diagonal[:, :, :, None]
    return blocks.astype(jnp.bfloat16)


def draw_left_ops(key, part):
    key = jax.random.fold_in(key, 11)
    key_noise, key_gain, key_rough = jax.random.split(key, 3)
    shape_full = (PAIRS, SECTORS, BLOCK, BLOCK)
    noise = jax.random.normal(key_noise, shape_full, jnp.float32)
    return build_blocks(noise, key_gain, key_rough)


def draw_right_ops(key, part):
    key = jax.random.fold_in(key, 23)
    key_noise, key_gain, key_rough = jax.random.split(key, 3)
    shape_full = (PAIRS, SECTORS, BLOCK, BLOCK)
    noise = jax.random.normal(key_noise, shape_full, jnp.float32)
    return build_blocks(noise, key_gain, key_rough)


def draw_block_sizes(key, part):
    key = jax.random.fold_in(key, 5)
    key_live, key_full = jax.random.split(key, 2)
    live_sizes = jax.random.randint(key_live, (SECTORS,), BLOCK // 4, BLOCK + 1, jnp.int32)
    full_at = jax.random.randint(key_full, (), 0, SECTORS, jnp.int32)
    places = jnp.arange(SECTORS, dtype=jnp.int32)
    return jnp.where(places == full_at, BLOCK, live_sizes).astype(jnp.int32)


def touch_ends(drawn, key, low, high):
    longest = drawn.shape.index(max(drawn.shape))
    spots = []
    for shift in (0, 1):
        where = [jax.random.randint(jax.random.fold_in(key, axis), (), 0, length) for axis, length in enumerate(drawn.shape)]
        where[longest] = (where[longest] + shift) % drawn.shape[longest]
        spots.append(tuple(where))
    return drawn.at[spots[0]].set(low).at[spots[1]].set(high)


def steps_of(stream_key, dims, cuts, smallest, high):
    level, own = 1.0, jax.random.fold_in(stream_key, 6)
    for axis_at, shards_of in cuts:
        steps = jnp.exp(jax.random.uniform(jax.random.fold_in(own, axis_at), (shards_of,), jnp.float32, smallest / len(cuts), high / len(cuts)))
        level = level * jnp.repeat(steps, dims[axis_at] // shards_of).reshape([-1 if axis == axis_at else 1 for axis in range(len(dims))])
    return level


def scatter_about(stream_key, dims, scale, bound, cuts=(), kind=jnp.bfloat16):
    array = scale * jax.random.normal(stream_key, dims, jnp.float32)
    if cuts:
        array = array * steps_of(stream_key, dims, cuts, -0.22, 0.18)
    return jnp.clip(array, -bound, bound).astype(kind)


def setup_inputs(seed: int = 0) -> dict:
    keys = jax.random.split(jax.random.key(seed), 6)
    wavefunction = scatter_about(keys[0], (SECTORS, BLOCK, BLOCK), 1.0, 6.0, ((0, 16),))
    left_ops = draw_left_ops(jax.random.fold_in(keys[5], 71), 0)
    right_ops = draw_right_ops(jax.random.fold_in(keys[5], 71), 0)
    charge = touch_ends(jax.random.randint(keys[3], (PAIRS,), 0, SECTORS), jax.random.fold_in(keys[3], 1), 0, SECTORS - 1).astype(jnp.int32)
    block_sizes = draw_block_sizes(jax.random.fold_in(keys[5], 71), 0)
    return dict(wavefunction=wavefunction, left_ops=left_ops, right_ops=right_ops, charge=charge, block_sizes=block_sizes)


def reference(wavefunction, left_ops, right_ops, charge, block_sizes):
    slot_positions = jnp.arange(BLOCK, dtype=jnp.int32)
    live_mask = (slot_positions[None, :] < block_sizes[:, None]).astype(wavefunction.dtype)
    masked = wavefunction * live_mask[:, :, None] * live_mask[:, None, :]
    targets = jnp.arange(SECTORS, dtype=jnp.int32)

    def one_pair(running, pair_items):
        left_sector_block, right_sector_block, offset = pair_items
        sources = ((targets + offset) % SECTORS).astype(jnp.int32)
        selected_rows = jnp.take(masked, sources, axis=0)
        split_pieces = jnp.einsum("khw,kwz->khz", left_sector_block.astype(jnp.float32), selected_rows.astype(jnp.float32)).astype(jnp.bfloat16)
        pair_contribution = jnp.einsum("ghu,giu->ghi", split_pieces.astype(jnp.float32), right_sector_block.astype(jnp.float32))
        return running + pair_contribution, None

    start_sum = jnp.zeros((SECTORS, BLOCK, BLOCK), jnp.float32)
    summed, _ = lax.scan(one_pair, start_sum, (left_ops, right_ops, charge))
    live_float = live_mask.astype(jnp.float32)
    sigma_full = summed * (PAIRS ** -0.5) * live_float[:, :, None] * live_float[:, None, :]
    masked_float = masked.astype(jnp.float32)
    ritz_value = jnp.sum(masked_float * sigma_full) / jnp.sum(masked_float * masked_float)
    sigma = sigma_full.astype(jnp.bfloat16)
    residual = (sigma_full - ritz_value * masked_float).astype(jnp.bfloat16)
    return sigma, residual
```

```python
import jax
import jax.numpy as jnp
from jax import lax
from jax.experimental import pallas as pl
from jax.experimental.pallas import tpu as pltpu
from jax.sharding import PartitionSpec as P

LANES = 128


def sigma_kernel(pairs, targets_here, sectors, rows, factor):
    def body(
        sec_ref, charge_ref, sizes_ref, psi_ref, left_ref, right_ref,
        out_ref, psi_buf, left_buf, right_buf, psi_sem, left_sem, right_sem,
    ):
        first = sec_ref[0] * targets_here
        block = left_buf.shape[-1]

        def source(p, k):
            return lax.rem(first + k + charge_ref[p], sectors)

        copies = []
        for p in range(pairs):
            left = pltpu.make_async_copy(left_ref.at[p], left_buf.at[p], left_sem.at[p])
            right = pltpu.make_async_copy(right_ref.at[p], right_buf.at[p], right_sem.at[p])
            blocks = [
                pltpu.make_async_copy(
                    psi_ref.at[source(p, k)], psi_buf.at[p * targets_here + k],
                    psi_sem.at[p * targets_here + k],
                )
                for k in range(targets_here)
            ]
            copies.append((left, right, blocks))
            for copy in (*blocks, left, right):
                copy.start()
        own = pairs * targets_here
        own_copies = [
            pltpu.make_async_copy(psi_ref.at[first + k], psi_buf.at[own + k], psi_sem.at[own + k])
            for k in range(targets_here)
        ]
        for copy in own_copies:
            copy.start()
        row = lax.broadcasted_iota(jnp.int32, (block, block), 0)
        column = lax.broadcasted_iota(jnp.int32, (block, block), 1)
        farthest = jnp.maximum(row, column)
        totals = [jnp.zeros((block, block), jnp.float32) for _ in range(targets_here)]
        for p, (left, right, blocks) in enumerate(copies):
            for copy in (*blocks, left, right):
                copy.wait()
            for k in range(targets_here):
                size = sizes_ref[source(p, k)]
                psi = jnp.where(farthest < size, psi_buf[p * targets_here + k], 0)
                half = jnp.dot(
                    left_buf[p, k], psi, preferred_element_type=jnp.float32
                ).astype(jnp.bfloat16)
                totals[k] += lax.dot_general(
                    half, right_buf[p, k], (((1,), (1,)), ((), ())),
                    preferred_element_type=jnp.float32,
                )
        correlation = jnp.zeros((1, 1), jnp.float32)
        for copy in own_copies:
            copy.wait()
        for k in range(targets_here):
            size = sizes_ref[first + k]
            total = totals[k] * factor
            psi = jnp.where(farthest < size, psi_buf[own + k], 0).astype(jnp.float32)
            correlation += jnp.sum(psi * total, keepdims=True)
            out_ref[:, k * rows : (k + 1) * rows, :block] = total.reshape(
                block // rows, rows, block
            ).astype(jnp.bfloat16)
        high = correlation.astype(jnp.bfloat16).astype(jnp.float32)
        middle = (correlation - high).astype(jnp.bfloat16).astype(jnp.float32)
        low = correlation - high - middle
        lane = lax.broadcasted_iota(jnp.int32, (targets_here * rows, LANES), 1)
        up = lax.broadcasted_iota(jnp.int32, (targets_here * rows, LANES), 0)
        words = jnp.where(lane == 0, high, jnp.where(lane == 1, middle, jnp.where(lane == 2, low, 0.0)))
        words = jnp.where(up == 0, words, 0.0).astype(jnp.bfloat16)
        out_ref[:, :, block:] = jnp.broadcast_to(words[None], (block // rows, *words.shape))

    return body


def local(wavefunction, left_ops, right_ops, charge, block_sizes):
    sec_count, block, _ = wavefunction.shape
    pairs = left_ops.shape[0]
    ops_count = lax.axis_size("ops")
    sec_total = lax.axis_size("sec")
    sectors = block_sizes.shape[0]
    rows = block // ops_count
    operator_slot = lax.axis_index("ops")
    sec_place = lax.axis_index("sec")
    factor = float(pairs * ops_count) ** (-0.5)

    gathered = lax.all_gather(wavefunction, "sec", axis=0, tiled=True)
    vmem, smem, anywhere = pltpu.VMEM, pltpu.SMEM, pl.ANY
    count = pairs * sec_count + sec_count
    pieces = pl.pallas_call(
        sigma_kernel(pairs, sec_count, sectors, rows, factor),
        out_shape=jax.ShapeDtypeStruct((ops_count, sec_count * rows, block + LANES), jnp.bfloat16),
        in_specs=[pl.BlockSpec(memory_space=smem)] * 3 + [pl.BlockSpec(memory_space=anywhere)] * 3,
        out_specs=pl.BlockSpec(memory_space=vmem),
        scratch_shapes=[
            pltpu.VMEM((count, block, block), jnp.bfloat16),
            pltpu.VMEM(left_ops.shape, jnp.bfloat16),
            pltpu.VMEM(right_ops.shape, jnp.bfloat16),
            pltpu.SemaphoreType.DMA((count,)),
            pltpu.SemaphoreType.DMA((pairs,)),
            pltpu.SemaphoreType.DMA((pairs,)),
        ],
        compiler_params=pltpu.CompilerParams(vmem_limit_bytes=32 * 2**20),
        cost_estimate=pl.CostEstimate(
            flops=4 * pairs * sec_count * block**3, bytes_accessed=7 * 2**20, transcendentals=0
        ),
    )(sec_place.reshape(1), charge, block_sizes, gathered, left_ops, right_ops)
    received = lax.all_to_all(pieces, "ops", 0, 0)
    summed = jnp.sum(received.astype(jnp.float32), axis=0)

    positions = jnp.arange(block, dtype=jnp.int32)
    own_sizes = lax.dynamic_slice_in_dim(block_sizes, sec_place * sec_count, sec_count, 0)
    live = (positions[None, :] < own_sizes[:, None]).astype(jnp.float32)
    masked = wavefunction.astype(jnp.float32) * live[:, :, None] * live[:, None, :]
    norm_here = jnp.sum(masked * masked)
    correlation_here = jnp.sum(summed[:, block:])
    both = jnp.stack([jnp.full((LANES,), correlation_here), jnp.full((LANES,), norm_here)])
    both = jnp.broadcast_to(both[None], (sec_total, 2, LANES))
    both = jnp.sum(lax.all_to_all(both, "sec", 0, 0), axis=0)
    ritz_value = both[0, 0] / both[1, 0]

    row_live = lax.dynamic_slice_in_dim(live, operator_slot * rows, rows, 1)
    sigma = summed[:, :block].reshape(sec_count, rows, block)
    sigma = sigma * row_live[:, :, None] * live[:, None, :]
    own_rows = lax.dynamic_slice_in_dim(masked, operator_slot * rows, rows, 1)
    return (
        sigma.astype(jnp.bfloat16),
        (sigma - ritz_value * own_rows).astype(jnp.bfloat16),
    )


def solution(mesh):
    placed = (
        P("sec", None, None),
        P("ops", "sec", None, None),
        P("ops", "sec", None, None),
        P("ops"),
        P(),
    )
    return jax.shard_map(
        local,
        mesh=mesh,
        in_specs=placed,
        out_specs=(P("sec", "ops", None), P("sec", "ops", None)),
        check_vma=False,
    )
```

```python
import jax
import jax.numpy as jnp
from jax import lax
from jax.experimental import pallas as pl
from jax.experimental.pallas import tpu as pltpu
from jax.sharding import PartitionSpec as P

LANES = 128
SUBLANES = 8
X_SIZE = 4
COLOURS = 4
VMEM_LIMIT = 56 * 2**20


def sigma_kernel(pairs, here, sectors, rows, factor):
    def body(
        place_ref, charge_ref, sizes_ref, psi_ref, near_ref, far_ref, near_other_ref, far_other_ref,
        left_ref, right_ref, out_ref, norm_ref, own_buf, psi_buf, left_buf, right_buf, half_buf,
        own_sem, psi_sem, left_sem, right_sem,
    ):
        sec, core, colour = place_ref[0], place_ref[1], place_ref[2]
        first = sec * here
        block = left_buf.shape[-1]
        quarter = block // COLOURS

        def fetch(p, k):
            source = lax.rem(first + k + charge_ref[p], sectors)
            place = lax.div(source, 2 * here) * here + lax.rem(source, here)
            other = lax.rem(lax.div(source, here), 2) != core
            slot = p * here + k

            def start(near, far):
                def copy(src, relative):
                    at = pl.multiple_of(lax.rem(colour + relative, COLOURS) * quarter, quarter)
                    pltpu.make_async_copy(
                        src, psi_buf.at[slot, pl.ds(at, quarter)], psi_sem.at[slot]
                    ).start()

                copy(near.at[place], 0)
                copy(far.at[place, pl.ds(0, quarter)], 1)
                copy(far.at[place, pl.ds(quarter, quarter)], 3)
                copy(far.at[place, pl.ds(2 * quarter, quarter)], 2)

            pl.when(other)(lambda: start(near_other_ref, far_other_ref))
            pl.when(jnp.logical_not(other))(lambda: start(near_ref, far_ref))

        own_copy = pltpu.make_async_copy(psi_ref, own_buf, own_sem)
        lefts = [
            pltpu.make_async_copy(left_ref.at[p], left_buf.at[p], left_sem.at[p])
            for p in range(pairs)
        ]
        rights = [
            pltpu.make_async_copy(
                right_ref.at[p, k], right_buf.at[k, :, pl.ds(p * block, block)],
                right_sem.at[p * here + k],
            )
            for p in range(pairs) for k in range(here)
        ]
        for p in range(pairs):
            lefts[p].start()
            for k in range(here):
                fetch(p, k)
        for copy in rights:
            copy.start()
        own_copy.start()
        row = lax.broadcasted_iota(jnp.int32, (block, block), 0)
        column = lax.broadcasted_iota(jnp.int32, (block, block), 1)
        farthest = jnp.maximum(row, column)
        for p in range(pairs):
            lefts[p].wait()
            for k in range(here):
                slot = p * here + k
                pltpu.make_async_copy(psi_buf.at[slot], psi_buf.at[slot], psi_sem.at[slot]).wait()
            for k in range(here):
                half_buf[k, :, p * block : (p + 1) * block] = jnp.dot(
                    left_buf[p, k], psi_buf[p * here + k], preferred_element_type=jnp.float32
                ).astype(jnp.bfloat16)
        for copy in rights:
            copy.wait()
        own_copy.wait()
        correlation = jnp.zeros((1, 1), jnp.float32)
        norm = jnp.zeros((1, 1), jnp.float32)
        for k in range(here):
            total = factor * lax.dot_general(
                half_buf[k], right_buf[k], (((1,), (1,)), ((), ())),
                preferred_element_type=jnp.float32,
            )
            psi = jnp.where(farthest < sizes_ref[first + k], own_buf[k], 0).astype(jnp.float32)
            correlation += jnp.sum(psi * total, keepdims=True)
            norm += jnp.sum(psi * psi, keepdims=True)
            out_ref[:, k * rows : (k + 1) * rows, :block] = total.reshape(
                block // rows, rows, block
            ).astype(jnp.bfloat16)
        high = correlation.astype(jnp.bfloat16).astype(jnp.float32)
        middle = (correlation - high).astype(jnp.bfloat16).astype(jnp.float32)
        low = correlation - high - middle
        lane = lax.broadcasted_iota(jnp.int32, (here * rows, LANES), 1)
        up = lax.broadcasted_iota(jnp.int32, (here * rows, LANES), 0)
        words = jnp.where(
            lane == 0, high, jnp.where(lane == 1, middle, jnp.where(lane == 2, low, 0.0))
        )
        words = jnp.where(up == 0, words, 0.0).astype(jnp.bfloat16)
        out_ref[:, :, block:] = jnp.broadcast_to(words[None], (block // rows, *words.shape))
        norm_ref[...] = jnp.broadcast_to(norm, norm_ref.shape)

    return body


def live_of(place_ref, sizes_ref, here, rows, block, k):
    size = sizes_ref[place_ref[0] * here + k]
    row = lax.broadcasted_iota(jnp.int32, (rows, block), 0) + place_ref[3] * rows
    column = lax.broadcasted_iota(jnp.int32, (rows, block), 1)
    return jnp.maximum(row, column) < size


def sum_kernel(here, rows, block):
    def body(place_ref, sizes_ref, received_ref, norm_ref, sigma_ref, wide_ref, both_ref):
        summed = jnp.sum(received_ref[...].astype(jnp.float32), axis=0)
        for k in range(here):
            part = summed[k * rows : (k + 1) * rows, :block]
            part = jnp.where(live_of(place_ref, sizes_ref, here, rows, block, k), part, 0.0)
            wide_ref[k] = part
            sigma_ref[k] = part.astype(jnp.bfloat16)
        correlation = jnp.sum(summed[:, block:], keepdims=True)
        up = lax.broadcasted_iota(jnp.int32, (SUBLANES, LANES), 0)
        both = jnp.where(up == 0, correlation, norm_ref[...])
        both_ref[...] = jnp.broadcast_to(both[None], both_ref.shape)

    return body


def residual_kernel(here, rows, block):
    def body(place_ref, sizes_ref, both_ref, wide_ref, own_ref, out_ref):
        both = jnp.sum(both_ref[...], axis=0)
        ritz_value = both[0:1, 0:1] / both[1:2, 0:1]
        for k in range(here):
            own = own_ref[k].astype(jnp.float32)
            own = jnp.where(live_of(place_ref, sizes_ref, here, rows, block, k), own, 0.0)
            out_ref[k] = (wide_ref[k] - ritz_value * own).astype(jnp.bfloat16)

    return body


def local(wavefunction, left_ops, right_ops, charge, block_sizes):
    here, block, _ = wavefunction.shape
    pairs = left_ops.shape[0]
    ops_count = lax.axis_size("ops")
    sec_total = lax.axis_size("sec")
    sectors = block_sizes.shape[0]
    rows = block // ops_count
    quarter = block // COLOURS
    operator_slot = lax.axis_index("ops")
    sec_place = lax.axis_index("sec")
    factor = float(pairs * ops_count) ** (-0.5)
    chips_z = sec_total // 2
    y_size = ops_count // X_SIZE
    colour = lax.rem(operator_slot % X_SIZE + 2 * (operator_slot // X_SIZE), COLOURS)
    place = jnp.stack([sec_place, sec_place % 2, colour, operator_slot])

    positions = jnp.arange(block, dtype=jnp.int32)
    own_sizes = lax.dynamic_slice_in_dim(block_sizes, sec_place * here, here, 0)
    live = positions[None, :] < own_sizes[:, None]
    own_quarter = lax.dynamic_slice_in_dim(wavefunction, colour * quarter, quarter, 1)
    row_live = lax.dynamic_slice_in_dim(live, colour * quarter, quarter, 1)
    own_quarter = jnp.where(row_live[:, :, None] & live[:, None, :], own_quarter, 0)
    spread = jnp.broadcast_to(own_quarter[None], (chips_z, *own_quarter.shape))
    same_core = [[2 * z + core for z in range(chips_z)] for core in range(2)]
    near = lax.all_to_all(spread, "sec", 0, 0, axis_index_groups=same_core)
    near = near.reshape(chips_z * here, quarter, block)

    def from_x(step):
        return [(y * X_SIZE + (x + step) % X_SIZE, y * X_SIZE + x)
                for y in range(y_size) for x in range(X_SIZE)]

    def from_y(step):
        return [((y + step) % y_size * X_SIZE + x, y * X_SIZE + x)
                for y in range(y_size) for x in range(X_SIZE)]

    swap = [(s, s ^ 1) for s in range(sec_total)]
    x_next = lax.ppermute(near, "ops", from_x(1))
    x_last = lax.ppermute(near, "ops", from_x(-1))
    y_next = lax.ppermute(near[:, : quarter // 2], "ops", from_y(1))
    y_last = lax.ppermute(near[:, quarter // 2 :], "ops", from_y(-1))
    near_other = lax.ppermute(near, "sec", swap)
    far = jnp.concatenate([x_next, x_last, y_next, y_last], axis=1)
    far_other = lax.ppermute(far, "sec", swap)

    smem = pl.BlockSpec(memory_space=pltpu.SMEM)
    vmem = pl.BlockSpec(memory_space=pltpu.VMEM)
    anywhere = pl.BlockSpec(memory_space=pl.ANY)
    count = pairs * here
    pieces, norm = pl.pallas_call(
        sigma_kernel(pairs, here, sectors, rows, factor),
        out_shape=(
            jax.ShapeDtypeStruct((ops_count, here * rows, block + LANES), jnp.bfloat16),
            jax.ShapeDtypeStruct((SUBLANES, LANES), jnp.float32),
        ),
        in_specs=[smem] * 3 + [anywhere] * 7,
        out_specs=(vmem, vmem),
        scratch_shapes=[
            pltpu.VMEM((here, block, block), jnp.bfloat16),
            pltpu.VMEM((count, block, block), jnp.bfloat16),
            pltpu.VMEM(left_ops.shape, jnp.bfloat16),
            pltpu.VMEM((here, block, pairs * block), jnp.bfloat16),
            pltpu.VMEM((here, block, pairs * block), jnp.bfloat16),
            pltpu.SemaphoreType.DMA,
            pltpu.SemaphoreType.DMA((count,)),
            pltpu.SemaphoreType.DMA((pairs,)),
            pltpu.SemaphoreType.DMA((count,)),
        ],
        compiler_params=pltpu.CompilerParams(vmem_limit_bytes=VMEM_LIMIT),
        cost_estimate=pl.CostEstimate(
            flops=4 * count * block**3, bytes_accessed=7 * 2**20, transcendentals=0
        ),
    )(place, charge, block_sizes, wavefunction, near, far, near_other, far_other, left_ops, right_ops)
    received = lax.all_to_all(pieces, "ops", 0, 0)

    sigma, wide, both = pl.pallas_call(
        sum_kernel(here, rows, block),
        out_shape=(
            jax.ShapeDtypeStruct((here, rows, block), jnp.bfloat16),
            jax.ShapeDtypeStruct((here, rows, block), jnp.float32),
            jax.ShapeDtypeStruct((sec_total, SUBLANES, LANES), jnp.float32),
        ),
        in_specs=[smem, smem, vmem, vmem],
        out_specs=(vmem, vmem, vmem),
    )(place, block_sizes, received, norm)
    both = lax.all_to_all(both, "sec", 0, 0)
    own_rows = lax.dynamic_slice_in_dim(wavefunction, operator_slot * rows, rows, 1)
    residual = pl.pallas_call(
        residual_kernel(here, rows, block),
        out_shape=jax.ShapeDtypeStruct((here, rows, block), jnp.bfloat16),
        in_specs=[smem, smem, vmem, vmem, vmem],
        out_specs=vmem,
    )(place, block_sizes, both, wide, own_rows)
    return sigma, residual


def solution(mesh):
    placed = (
        P("sec", None, None),
        P("ops", "sec", None, None),
        P("ops", "sec", None, None),
        P("ops"),
        P(),
    )
    return jax.shard_map(
        local,
        mesh=mesh,
        in_specs=placed,
        out_specs=(P("sec", "ops", None), P("sec", "ops", None)),
        check_vma=False,
    )
```

```python
import jax
import jax.numpy as jnp
from jax import lax
from jax.experimental import pallas as pl
from jax.experimental.pallas import tpu as pltpu
from jax.sharding import PartitionSpec as P

LANES = 128
SUBLANES = 8
X_SIZE = 4
COLOURS = 4
VMEM_LIMIT = 24 * 2**20
SMALL = pltpu.CompilerParams(vmem_limit_bytes=4 * 2**20)


def colour_of(slot):
    return lax.rem(lax.rem(slot, X_SIZE) + 2 * lax.div(slot, X_SIZE), COLOURS)


def spread_kernel(sizes_ref, psi_ref, out_ref, buf, sem):
    copies, here, quarter, block = out_ref.shape
    first = lax.axis_index("sec") * here
    start = pl.multiple_of(colour_of(lax.axis_index("ops")) * quarter, quarter)
    copy = pltpu.make_async_copy(psi_ref.at[:, pl.ds(start, quarter)], buf, sem)
    copy.start()
    row = lax.broadcasted_iota(jnp.int32, (quarter, block), 0) + start
    farthest = jnp.maximum(row, lax.broadcasted_iota(jnp.int32, (quarter, block), 1))
    copy.wait()
    for k in range(here):
        part = jnp.where(farthest < sizes_ref[first + k], buf[k], 0)
        for copy_at in range(copies):
            out_ref[copy_at, k] = part


def sigma_kernel(sectors, rows, factor):
    def body(
        charge_ref, sizes_ref, psi_ref, mine_ref, other_ref, left_ref, right_ref,
        out_ref, norm_ref, own_ref, live_ref, half_buf, own_buf,
    ):
        pairs, here, block, _ = left_ref.shape
        sec = lax.axis_index("sec")
        first = sec * here
        start = pl.multiple_of(lax.axis_index("ops") * rows, rows)
        core = lax.rem(sec, 2)
        for p in range(pairs):
            for k in range(here):
                source = lax.rem(first + k + charge_ref[p], sectors)
                place = lax.div(source, 2 * here) * here + lax.rem(source, here)
                across = lax.rem(lax.div(source, here), 2) != core
                psi = jnp.where(across, other_ref[place], mine_ref[place])
                half_buf[k, :, p * block : (p + 1) * block] = jnp.dot(
                    left_ref[p, k], psi, preferred_element_type=jnp.float32
                ).astype(jnp.bfloat16)
        row = lax.broadcasted_iota(jnp.int32, (block, block), 0)
        column = lax.broadcasted_iota(jnp.int32, (block, block), 1)
        farthest = jnp.maximum(row, column)
        part_row = lax.broadcasted_iota(jnp.int32, (rows, block), 0) + start
        part_farthest = jnp.maximum(part_row, lax.broadcasted_iota(jnp.int32, (rows, block), 1))
        correlation = jnp.zeros((1, 1), jnp.float32)
        norm = jnp.zeros((1, 1), jnp.float32)
        for k in range(here):
            size = sizes_ref[first + k]
            total = jnp.zeros((block, block), jnp.float32)
            for p in range(pairs):
                total += lax.dot_general(
                    half_buf[k, :, p * block : (p + 1) * block], right_ref[p, k],
                    (((1,), (1,)), ((), ())), preferred_element_type=jnp.float32,
                )
            total = total * factor
            psi = jnp.where(farthest < size, psi_ref[k], 0).astype(jnp.float32)
            own_buf[k] = psi
            correlation += jnp.sum(psi * total, keepdims=True)
            norm += jnp.sum(psi * psi, keepdims=True)
            out_ref[:, k * rows : (k + 1) * rows, :block] = total.reshape(
                block // rows, rows, block
            ).astype(jnp.bfloat16)
            own_ref[k] = own_buf[k, pl.ds(start, rows)]
            live_ref[k] = jnp.where(part_farthest < size, 1.0, 0.0)
        high = correlation.astype(jnp.bfloat16).astype(jnp.float32)
        middle = (correlation - high).astype(jnp.bfloat16).astype(jnp.float32)
        low = correlation - high - middle
        lane = lax.broadcasted_iota(jnp.int32, (here * rows, LANES), 1)
        up = lax.broadcasted_iota(jnp.int32, (here * rows, LANES), 0)
        words = jnp.where(
            lane == 0, high, jnp.where(lane == 1, middle, jnp.where(lane == 2, low, 0.0))
        )
        words = jnp.where(up == 0, words, 0.0).astype(jnp.bfloat16)
        out_ref[:, :, block:] = jnp.broadcast_to(words[None], (block // rows, *words.shape))
        norm_ref[...] = jnp.broadcast_to(norm, norm_ref.shape)

    return body


def sum_kernel(received_ref, norm_ref, live_ref, sigma_ref, wide_ref, both_ref):
    here, rows, block = wide_ref.shape
    summed = jnp.sum(received_ref[...].astype(jnp.float32), axis=0)
    correlation = jnp.sum(summed[:, block:], keepdims=True)
    up = lax.broadcasted_iota(jnp.int32, both_ref.shape[1:], 0)
    both = jnp.where(up == 0, correlation, norm_ref[...])
    both_ref[...] = jnp.broadcast_to(both[None], both_ref.shape)
    for k in range(here):
        part = jnp.where(live_ref[k] > 0, summed[k * rows : (k + 1) * rows, :block], 0.0)
        wide_ref[k] = part
        sigma_ref[k] = part.astype(jnp.bfloat16)


def residual_kernel(both_ref, wide_ref, own_ref, out_ref):
    both = jnp.sum(both_ref[...], axis=0)
    ritz_value = both[0:1, 0:1] / both[1:2, 0:1]
    for k in range(wide_ref.shape[0]):
        out_ref[k] = (wide_ref[k] - ritz_value * own_ref[k]).astype(jnp.bfloat16)


def local(wavefunction, left_ops, right_ops, charge, block_sizes):
    here, block, _ = wavefunction.shape
    pairs = left_ops.shape[0]
    ops_count = lax.axis_size("ops")
    sec_total = lax.axis_size("sec")
    sectors = block_sizes.shape[0]
    rows = block // ops_count
    quarter = block // COLOURS
    factor = float(pairs * ops_count) ** (-0.5)
    chips_z = sec_total // 2
    y_size = ops_count // X_SIZE
    colour = colour_of(lax.axis_index("ops"))
    smem = pl.BlockSpec(memory_space=pltpu.SMEM)
    vmem = pl.BlockSpec(memory_space=pltpu.VMEM)
    bf16, f32 = jnp.bfloat16, jnp.float32

    spread = pl.pallas_call(
        spread_kernel,
        out_shape=jax.ShapeDtypeStruct((chips_z, here, quarter, block), bf16),
        in_specs=[smem, pl.BlockSpec(memory_space=pl.ANY)],
        out_specs=vmem,
        scratch_shapes=[pltpu.VMEM((here, quarter, block), bf16), pltpu.SemaphoreType.DMA],
        compiler_params=SMALL,
    )(block_sizes, wavefunction)
    same_core = [[2 * z + core for z in range(chips_z)] for core in range(2)]
    near = lax.all_to_all(spread, "sec", 0, 0, axis_index_groups=same_core)
    near = near.reshape(chips_z * here, quarter, block)

    def from_x(step):
        return [(y * X_SIZE + (x + step) % X_SIZE, y * X_SIZE + x)
                for y in range(y_size) for x in range(X_SIZE)]

    def from_y(step):
        return [((y + step) % y_size * X_SIZE + x, y * X_SIZE + x)
                for y in range(y_size) for x in range(X_SIZE)]

    x_next = lax.ppermute(near, "ops", from_x(1))
    x_last = lax.ppermute(near, "ops", from_x(-1))
    y_next = lax.ppermute(near[:, : quarter // 2], "ops", from_y(1))
    y_last = lax.ppermute(near[:, quarter // 2 :], "ops", from_y(-1))
    mine = jnp.zeros((chips_z * here, COLOURS, quarter, block), bf16)
    for piece, relative, at in (
        (near, 0, 0), (x_next, 1, 0), (x_last, 3, 0), (y_next, 2, 0), (y_last, 2, quarter // 2)
    ):
        where = (0, lax.rem(colour + relative, COLOURS), at, 0)
        mine = lax.dynamic_update_slice(mine, piece[:, None], where)
    mine = mine.reshape(chips_z * here, block, block)
    other = lax.ppermute(mine, "sec", [(s, s ^ 1) for s in range(sec_total)])

    part = (here, rows, block)
    pieces, norm, own_rows, live = pl.pallas_call(
        sigma_kernel(sectors, rows, factor),
        out_shape=(
            jax.ShapeDtypeStruct((ops_count, here * rows, block + LANES), bf16),
            jax.ShapeDtypeStruct((SUBLANES, LANES), f32),
            jax.ShapeDtypeStruct(part, f32),
            jax.ShapeDtypeStruct(part, f32),
        ),
        in_specs=[smem] * 2 + [vmem] * 5,
        out_specs=(vmem,) * 4,
        scratch_shapes=[
            pltpu.VMEM((here, block, pairs * block), bf16),
            pltpu.VMEM((here, block, block), f32),
        ],
        compiler_params=pltpu.CompilerParams(vmem_limit_bytes=VMEM_LIMIT),
        cost_estimate=pl.CostEstimate(
            flops=4 * pairs * here * block**3, bytes_accessed=2**20, transcendentals=0
        ),
    )(charge, block_sizes, wavefunction, mine, other, left_ops, right_ops)
    received = lax.all_to_all(pieces, "ops", 0, 0)

    sigma, wide, both = pl.pallas_call(
        sum_kernel,
        out_shape=(
            jax.ShapeDtypeStruct(part, bf16),
            jax.ShapeDtypeStruct(part, f32),
            jax.ShapeDtypeStruct((sec_total, SUBLANES, LANES), f32),
        ),
        in_specs=[vmem] * 3,
        out_specs=(vmem,) * 3,
        compiler_params=SMALL,
    )(received, norm, live)
    both = lax.all_to_all(both, "sec", 0, 0)
    residual = pl.pallas_call(
        residual_kernel,
        out_shape=jax.ShapeDtypeStruct(part, bf16),
        in_specs=[vmem] * 3,
        out_specs=vmem,
        compiler_params=SMALL,
    )(both, wide, own_rows)
    return sigma, residual


def solution(mesh):
    placed = (
        P("sec", None, None),
        P("ops", "sec", None, None),
        P("ops", "sec", None, None),
        P("ops"),
        P(),
    )
    return jax.shard_map(
        local,
        mesh=mesh,
        in_specs=placed,
        out_specs=(P("sec", "ops", None), P("sec", "ops", None)),
        check_vma=False,
    )
```

```python
import jax
import jax.numpy as jnp
from jax import lax
from jax.experimental import pallas as pl
from jax.experimental.pallas import tpu as pltpu
from jax.sharding import PartitionSpec as P

LANES = 128
SUBLANES = 8
X_SIZE = 4
COLOURS = 4
VMEM_LIMIT = 24 * 2**20
SMALL = pltpu.CompilerParams(vmem_limit_bytes=4 * 2**20)


def colour_of(slot):
    return lax.rem(lax.rem(slot, X_SIZE) + 2 * lax.div(slot, X_SIZE), COLOURS)


def sigma_kernel(sectors, rows, factor):
    def body(
        charge_ref, sizes_ref, live_all_ref, psi_ref, mine_ref, other_ref, left_ref, right_ref,
        out_ref, norm_ref, own_ref, live_ref, half_buf, own_buf,
    ):
        pairs, here, block, _ = left_ref.shape
        sec = lax.axis_index("sec")
        first = sec * here
        start = pl.multiple_of(lax.axis_index("ops") * rows, rows)
        core = lax.rem(sec, 2)
        for p in range(pairs):
            for k in range(here):
                source = lax.rem(first + k + charge_ref[p], sectors)
                place = lax.div(source, 2 * here) * here + lax.rem(source, here)
                across = lax.rem(lax.div(source, here), 2) != core
                psi = jnp.where(across, other_ref[place], mine_ref[place])
                live = live_all_ref[pl.ds(source, 1), :]
                left = left_ref[p, k] * live.astype(jnp.bfloat16)
                half = jnp.dot(left, psi, preferred_element_type=jnp.float32) * live
                half_buf[k, :, p * block : (p + 1) * block] = half.astype(jnp.bfloat16)
        row = lax.broadcasted_iota(jnp.int32, (block, block), 0)
        column = lax.broadcasted_iota(jnp.int32, (block, block), 1)
        farthest = jnp.maximum(row, column)
        part_row = lax.broadcasted_iota(jnp.int32, (rows, block), 0) + start
        part_farthest = jnp.maximum(part_row, lax.broadcasted_iota(jnp.int32, (rows, block), 1))
        correlation = jnp.zeros((1, 1), jnp.float32)
        norm = jnp.zeros((1, 1), jnp.float32)
        for k in range(here):
            size = sizes_ref[first + k]
            total = jnp.zeros((block, block), jnp.float32)
            for p in range(pairs):
                total += lax.dot_general(
                    half_buf[k, :, p * block : (p + 1) * block], right_ref[p, k],
                    (((1,), (1,)), ((), ())), preferred_element_type=jnp.float32,
                )
            total = total * factor
            psi = jnp.where(farthest < size, psi_ref[k], 0).astype(jnp.float32)
            own_buf[k] = psi
            correlation += jnp.sum(psi * total, keepdims=True)
            norm += jnp.sum(psi * psi, keepdims=True)
            cut = total.reshape(block // rows, rows, block).astype(jnp.bfloat16)
            for part in range(block // LANES):
                at = (part * here + k) * rows
                out_ref[:, at : at + rows, :] = cut[:, :, part * LANES : (part + 1) * LANES]
            own_ref[k] = own_buf[k, pl.ds(start, rows)]
            live_ref[k] = jnp.where(part_farthest < size, 1.0, 0.0)
        high = correlation.astype(jnp.bfloat16).astype(jnp.float32)
        middle = (correlation - high).astype(jnp.bfloat16).astype(jnp.float32)
        low = correlation - high - middle
        lane = lax.broadcasted_iota(jnp.int32, (rows, LANES), 1)
        up = lax.broadcasted_iota(jnp.int32, (rows, LANES), 0)
        words = jnp.where(
            lane == 0, high, jnp.where(lane == 1, middle, jnp.where(lane == 2, low, 0.0))
        )
        words = jnp.where(up == 0, words, 0.0).astype(jnp.bfloat16)
        body_rows = here * rows * (block // LANES)
        out_ref[:, body_rows:, :] = jnp.broadcast_to(words[None], (block // rows, *words.shape))
        norm_ref[...] = jnp.broadcast_to(norm, norm_ref.shape)

    return body


def sum_kernel(received_ref, norm_ref, live_ref, sigma_ref, wide_ref, both_ref):
    here, rows, block = wide_ref.shape
    summed = jnp.sum(received_ref[...].astype(jnp.float32), axis=0)
    parts = block // LANES
    correlation = jnp.sum(summed[parts * here * rows :], keepdims=True)
    up = lax.broadcasted_iota(jnp.int32, both_ref.shape[1:], 0)
    both = jnp.where(up == 0, correlation, norm_ref[...])
    both_ref[...] = jnp.broadcast_to(both[None], both_ref.shape)
    for k in range(here):
        for part in range(parts):
            at, lanes = (part * here + k) * rows, slice(part * LANES, (part + 1) * LANES)
            kept = jnp.where(live_ref[k, :, lanes] > 0, summed[at : at + rows], 0.0)
            wide_ref[k, :, lanes] = kept
            sigma_ref[k, :, lanes] = kept.astype(jnp.bfloat16)


def residual_kernel(both_ref, wide_ref, own_ref, out_ref):
    both = jnp.sum(both_ref[...], axis=0)
    ritz_value = both[0:1, 0:1] / both[1:2, 0:1]
    for k in range(wide_ref.shape[0]):
        out_ref[k] = (wide_ref[k] - ritz_value * own_ref[k]).astype(jnp.bfloat16)


def local(wavefunction, left_ops, right_ops, charge, block_sizes):
    here, block, _ = wavefunction.shape
    pairs = left_ops.shape[0]
    ops_count = lax.axis_size("ops")
    sec_total = lax.axis_size("sec")
    sectors = block_sizes.shape[0]
    rows = block // ops_count
    quarter = block // COLOURS
    factor = float(pairs * ops_count) ** (-0.5)
    chips_z = sec_total // 2
    y_size = ops_count // X_SIZE
    colour = colour_of(lax.axis_index("ops"))
    smem = pl.BlockSpec(memory_space=pltpu.SMEM)
    vmem = pl.BlockSpec(memory_space=pltpu.VMEM)
    bf16, f32 = jnp.bfloat16, jnp.float32

    own_quarter = lax.dynamic_slice_in_dim(wavefunction, colour * quarter, quarter, 1)
    spread = jnp.broadcast_to(own_quarter[None], (chips_z, *own_quarter.shape))
    positions = jnp.arange(block, dtype=jnp.int32)
    live_all = (positions[None, :] < block_sizes[:, None]).astype(f32)
    same_core = [[2 * z + core for z in range(chips_z)] for core in range(2)]
    near = lax.all_to_all(spread, "sec", 0, 0, axis_index_groups=same_core)
    near = near.reshape(chips_z * here, quarter, block)

    def from_x(step):
        return [(y * X_SIZE + (x + step) % X_SIZE, y * X_SIZE + x)
                for y in range(y_size) for x in range(X_SIZE)]

    def from_y(step):
        return [((y + step) % y_size * X_SIZE + x, y * X_SIZE + x)
                for y in range(y_size) for x in range(X_SIZE)]

    x_next = lax.ppermute(near, "ops", from_x(1))
    x_last = lax.ppermute(near, "ops", from_x(-1))
    y_next = lax.ppermute(near[:, : quarter // 2], "ops", from_y(1))
    y_last = lax.ppermute(near[:, quarter // 2 :], "ops", from_y(-1))
    mine = jnp.zeros((chips_z * here, COLOURS, quarter, block), bf16)
    for piece, relative, at in (
        (near, 0, 0), (x_next, 1, 0), (x_last, 3, 0), (y_next, 2, 0), (y_last, 2, quarter // 2)
    ):
        where = (0, lax.rem(colour + relative, COLOURS), at, 0)
        mine = lax.dynamic_update_slice(mine, piece[:, None], where)
    mine = mine.reshape(chips_z * here, block, block)
    other = lax.ppermute(mine, "sec", [(s, s ^ 1) for s in range(sec_total)])

    part = (here, rows, block)
    pack_rows = here * rows * (block // LANES) + rows
    pieces, norm, own_rows, live = pl.pallas_call(
        sigma_kernel(sectors, rows, factor),
        out_shape=(
            jax.ShapeDtypeStruct((ops_count, pack_rows, LANES), bf16),
            jax.ShapeDtypeStruct((SUBLANES, LANES), f32),
            jax.ShapeDtypeStruct(part, f32),
            jax.ShapeDtypeStruct(part, f32),
        ),
        in_specs=[smem] * 2 + [vmem] * 6,
        out_specs=(vmem,) * 4,
        scratch_shapes=[
            pltpu.VMEM((here, block, pairs * block), bf16),
            pltpu.VMEM((here, block, block), f32),
        ],
        compiler_params=pltpu.CompilerParams(vmem_limit_bytes=VMEM_LIMIT),
        cost_estimate=pl.CostEstimate(
            flops=4 * pairs * here * block**3, bytes_accessed=2**20, transcendentals=0
        ),
    )(charge, block_sizes, live_all, wavefunction, mine, other, left_ops, right_ops)
    received = lax.all_to_all(pieces, "ops", 0, 0)

    sigma, wide, both = pl.pallas_call(
        sum_kernel,
        out_shape=(
            jax.ShapeDtypeStruct(part, bf16),
            jax.ShapeDtypeStruct(part, f32),
            jax.ShapeDtypeStruct((sec_total, SUBLANES, LANES), f32),
        ),
        in_specs=[vmem] * 3,
        out_specs=(vmem,) * 3,
        compiler_params=SMALL,
    )(received, norm, live)
    both = lax.all_to_all(both, "sec", 0, 0)
    residual = pl.pallas_call(
        residual_kernel,
        out_shape=jax.ShapeDtypeStruct(part, bf16),
        in_specs=[vmem] * 3,
        out_specs=vmem,
        compiler_params=SMALL,
    )(both, wide, own_rows)
    return sigma, residual


def solution(mesh):
    placed = (
        P("sec", None, None),
        P("ops", "sec", None, None),
        P("ops", "sec", None, None),
        P("ops"),
        P(),
    )
    return jax.shard_map(
        local,
        mesh=mesh,
        in_specs=placed,
        out_specs=(P("sec", "ops", None), P("sec", "ops", None)),
        check_vma=False,
    )
```

```python
import jax
import jax.numpy as jnp
from jax import lax
from jax.experimental import pallas as pl
from jax.experimental.pallas import tpu as pltpu
from jax.sharding import PartitionSpec as P

LANES = 128
SUBLANES = 8
X_SIZE = 4
COLOURS = 4
VMEM_LIMIT = 24 * 2**20
SMALL = pltpu.CompilerParams(vmem_limit_bytes=4 * 2**20)


def colour_of(slot):
    return lax.rem(lax.rem(slot, X_SIZE) + 2 * lax.div(slot, X_SIZE), COLOURS)


def sigma_kernel(sectors, rows, factor):
    def body(
        charge_ref, sizes_ref, mine_ref, other_ref, left_ref, right_ref,
        out_ref, norm_ref, own_ref, live_ref, half_buf, own_buf,
    ):
        pairs, here, block, _ = left_ref.shape
        sec = lax.axis_index("sec")
        first = sec * here
        start = pl.multiple_of(lax.axis_index("ops") * rows, rows)
        core = lax.rem(sec, 2)
        lane = lax.broadcasted_iota(jnp.int32, (1, block), 1)

        def block_of(source):
            mine, other = mine_ref[source], other_ref[source]
            upper = jnp.where(core == 0, mine, other)
            lower = jnp.where(core == 0, other, mine)
            eighths = [part[q] for q in range(COLOURS) for part in (upper, lower)]
            return jnp.concatenate(eighths, axis=0)

        for p in range(pairs):
            for k in range(here):
                source = lax.rem(first + k + charge_ref[p], sectors)
                live = jnp.where(lane < sizes_ref[source], 1.0, 0.0)
                left = left_ref[p, k] * live.astype(jnp.bfloat16)
                half = jnp.dot(left, block_of(source), preferred_element_type=jnp.float32) * live
                half_buf[k, :, p * block : (p + 1) * block] = half.astype(jnp.bfloat16)
        row = lax.broadcasted_iota(jnp.int32, (block, block), 0)
        column = lax.broadcasted_iota(jnp.int32, (block, block), 1)
        farthest = jnp.maximum(row, column)
        part_row = lax.broadcasted_iota(jnp.int32, (rows, block), 0) + start
        part_farthest = jnp.maximum(part_row, lax.broadcasted_iota(jnp.int32, (rows, block), 1))
        correlation = jnp.zeros((1, 1), jnp.float32)
        norm = jnp.zeros((1, 1), jnp.float32)
        for k in range(here):
            size = sizes_ref[first + k]
            total = jnp.zeros((block, block), jnp.float32)
            for p in range(pairs):
                total += lax.dot_general(
                    half_buf[k, :, p * block : (p + 1) * block], right_ref[p, k],
                    (((1,), (1,)), ((), ())), preferred_element_type=jnp.float32,
                )
            total = total * factor
            psi = jnp.where(farthest < size, block_of(first + k), 0).astype(jnp.float32)
            own_buf[k] = psi
            correlation += jnp.sum(psi * total, keepdims=True)
            norm += jnp.sum(psi * psi, keepdims=True)
            cut = total.reshape(block // rows, rows, block).astype(jnp.bfloat16)
            for part in range(block // LANES):
                at = (part * here + k) * rows
                out_ref[:, at : at + rows, :] = cut[:, :, part * LANES : (part + 1) * LANES]
            own_ref[k] = own_buf[k, pl.ds(start, rows)]
            live_ref[k] = jnp.where(part_farthest < size, 1.0, 0.0)
        high = correlation.astype(jnp.bfloat16).astype(jnp.float32)
        middle = (correlation - high).astype(jnp.bfloat16).astype(jnp.float32)
        low = correlation - high - middle
        lane = lax.broadcasted_iota(jnp.int32, (rows, LANES), 1)
        up = lax.broadcasted_iota(jnp.int32, (rows, LANES), 0)
        words = jnp.where(
            lane == 0, high, jnp.where(lane == 1, middle, jnp.where(lane == 2, low, 0.0))
        )
        words = jnp.where(up == 0, words, 0.0).astype(jnp.bfloat16)
        body_rows = here * rows * (block // LANES)
        out_ref[:, body_rows:, :] = jnp.broadcast_to(words[None], (block // rows, *words.shape))
        norm_ref[...] = jnp.broadcast_to(norm, norm_ref.shape)

    return body


def sum_kernel(received_ref, norm_ref, live_ref, sigma_ref, wide_ref, both_ref):
    here, rows, block = wide_ref.shape
    summed = jnp.sum(received_ref[...].astype(jnp.float32), axis=0)
    parts = block // LANES
    correlation = jnp.sum(summed[parts * here * rows :], keepdims=True)
    up = lax.broadcasted_iota(jnp.int32, both_ref.shape[1:], 0)
    both = jnp.where(up == 0, correlation, norm_ref[...])
    both_ref[...] = jnp.broadcast_to(both[None], both_ref.shape)
    for k in range(here):
        for part in range(parts):
            at, lanes = (part * here + k) * rows, slice(part * LANES, (part + 1) * LANES)
            kept = jnp.where(live_ref[k, :, lanes] > 0, summed[at : at + rows], 0.0)
            wide_ref[k, :, lanes] = kept
            sigma_ref[k, :, lanes] = kept.astype(jnp.bfloat16)


def residual_kernel(both_ref, wide_ref, own_ref, out_ref):
    both = jnp.sum(both_ref[...], axis=0)
    ritz_value = both[0:1, 0:1] / both[1:2, 0:1]
    for k in range(wide_ref.shape[0]):
        out_ref[k] = (wide_ref[k] - ritz_value * own_ref[k]).astype(jnp.bfloat16)


def local(wavefunction, left_ops, right_ops, charge, block_sizes):
    here, block, _ = wavefunction.shape
    pairs = left_ops.shape[0]
    ops_count = lax.axis_size("ops")
    sec_total = lax.axis_size("sec")
    sectors = block_sizes.shape[0]
    rows = block // ops_count
    quarter = block // COLOURS
    eighth = quarter // 2
    factor = float(pairs * ops_count) ** (-0.5)
    y_size = ops_count // X_SIZE
    colour = colour_of(lax.axis_index("ops"))
    smem = pl.BlockSpec(memory_space=pltpu.SMEM)
    vmem = pl.BlockSpec(memory_space=pltpu.VMEM)
    bf16, f32 = jnp.bfloat16, jnp.float32

    core = lax.axis_index("sec") % 2
    own = lax.dynamic_slice_in_dim(wavefunction, colour * quarter, quarter, 1)
    halves = own.reshape(here, 2, eighth, block).transpose(1, 0, 2, 3)
    spread = jnp.broadcast_to(halves[None], (sec_total // 2, *halves.shape))
    spread = spread.reshape(sec_total, here, eighth, block)
    own = lax.all_to_all(spread, "sec", 0, 0).reshape(sectors, eighth, block)

    def device(x, y, s):
        return ((y % y_size) * X_SIZE + x % X_SIZE) * sec_total + s

    def fetch(step_x, step_y):
        pairs = []
        for y in range(y_size):
            for x in range(X_SIZE):
                for s in range(sec_total):
                    way = 1 - 2 * (s % 2)
                    pairs.append((device(x + way * step_x, y + way * step_y, s), device(x, y, s)))
        return lax.ppermute(own, ("ops", "sec"), pairs)

    swap = [(s, s ^ 1) for s in range(sec_total)]
    mine = jnp.zeros((sectors, COLOURS, eighth, block), bf16)
    other = mine
    pieces = ((own, 0, 0), (fetch(1, 0), 1, 2), (fetch(0, 1), 2, 0), (fetch(-1, 0), 3, -2))
    for piece, relative, way in pieces:
        where = (0, lax.rem(colour + relative + way * core, COLOURS), 0, 0)
        mine = lax.dynamic_update_slice(mine, piece[:, None], where)
        where = (0, lax.rem(colour + relative + way * (1 - core), COLOURS), 0, 0)
        other = lax.dynamic_update_slice(other, lax.ppermute(piece, "sec", swap)[:, None], where)

    part = (here, rows, block)
    pack_rows = here * rows * (block // LANES) + rows
    pieces, norm, own_rows, live = pl.pallas_call(
        sigma_kernel(sectors, rows, factor),
        out_shape=(
            jax.ShapeDtypeStruct((ops_count, pack_rows, LANES), bf16),
            jax.ShapeDtypeStruct((SUBLANES, LANES), f32),
            jax.ShapeDtypeStruct(part, f32),
            jax.ShapeDtypeStruct(part, f32),
        ),
        in_specs=[smem] * 2 + [vmem] * 4,
        out_specs=(vmem,) * 4,
        scratch_shapes=[
            pltpu.VMEM((here, block, pairs * block), bf16),
            pltpu.VMEM((here, block, block), f32),
        ],
        compiler_params=pltpu.CompilerParams(vmem_limit_bytes=VMEM_LIMIT),
        cost_estimate=pl.CostEstimate(
            flops=4 * pairs * here * block**3, bytes_accessed=2**20, transcendentals=0
        ),
    )(charge, block_sizes, mine, other, left_ops, right_ops)
    received = lax.all_to_all(pieces, "ops", 0, 0)

    sigma, wide, both = pl.pallas_call(
        sum_kernel,
        out_shape=(
            jax.ShapeDtypeStruct(part, bf16),
            jax.ShapeDtypeStruct(part, f32),
            jax.ShapeDtypeStruct((sec_total, SUBLANES, LANES), f32),
        ),
        in_specs=[vmem] * 3,
        out_specs=(vmem,) * 3,
        compiler_params=SMALL,
    )(received, norm, live)
    both = lax.all_to_all(both, "sec", 0, 0)
    residual = pl.pallas_call(
        residual_kernel,
        out_shape=jax.ShapeDtypeStruct(part, bf16),
        in_specs=[vmem] * 3,
        out_specs=vmem,
        compiler_params=SMALL,
    )(both, wide, own_rows)
    return sigma, residual


def solution(mesh):
    placed = (
        P("sec", None, None),
        P("ops", "sec", None, None),
        P("ops", "sec", None, None),
        P("ops"),
        P(),
    )
    return jax.shard_map(
        local,
        mesh=mesh,
        in_specs=placed,
        out_specs=(P("sec", "ops", None), P("sec", "ops", None)),
        check_vma=False,
    )
```

```python
import jax
import jax.numpy as jnp
from jax import lax
from jax.experimental import pallas as pl
from jax.experimental.pallas import tpu as pltpu
from jax.sharding import PartitionSpec as P

LANES = 128
SUBLANES = 8
X_SIZE = 4
COLOURS = 4
VMEM_LIMIT = 24 * 2**20
SMALL = pltpu.CompilerParams(vmem_limit_bytes=4 * 2**20)


def colour_of(slot):
    return lax.rem(2 * lax.rem(slot, X_SIZE) + lax.div(slot, X_SIZE), COLOURS)


def sigma_kernel(sectors, rows, factor):
    def body(
        charge_ref, sizes_ref, mine_ref, other_ref, left_ref, right_ref,
        out_ref, norm_ref, own_ref, live_ref, half_buf, own_buf,
    ):
        pairs, here, block, _ = left_ref.shape
        sec = lax.axis_index("sec")
        first = sec * here
        start = pl.multiple_of(lax.axis_index("ops") * rows, rows)
        core = lax.rem(sec, 2)
        lane = lax.broadcasted_iota(jnp.int32, (1, block), 1)

        def block_of(source):
            mine, other = mine_ref[source], other_ref[source]
            upper = jnp.where(core == 0, mine, other)
            lower = jnp.where(core == 0, other, mine)
            eighths = [part[q] for q in range(COLOURS) for part in (upper, lower)]
            return jnp.concatenate(eighths, axis=0)

        for p in range(pairs):
            for k in range(here):
                source = lax.rem(first + k + charge_ref[p], sectors)
                live = jnp.where(lane < sizes_ref[source], 1.0, 0.0)
                left = left_ref[p, k] * live.astype(jnp.bfloat16)
                half = jnp.dot(left, block_of(source), preferred_element_type=jnp.float32) * live
                half_buf[k, :, p * block : (p + 1) * block] = half.astype(jnp.bfloat16)
        row = lax.broadcasted_iota(jnp.int32, (block, block), 0)
        column = lax.broadcasted_iota(jnp.int32, (block, block), 1)
        farthest = jnp.maximum(row, column)
        part_row = lax.broadcasted_iota(jnp.int32, (rows, block), 0) + start
        part_farthest = jnp.maximum(part_row, lax.broadcasted_iota(jnp.int32, (rows, block), 1))
        correlation = jnp.zeros((1, 1), jnp.float32)
        norm = jnp.zeros((1, 1), jnp.float32)
        for k in range(here):
            size = sizes_ref[first + k]
            total = jnp.zeros((block, block), jnp.float32)
            for p in range(pairs):
                total += lax.dot_general(
                    half_buf[k, :, p * block : (p + 1) * block], right_ref[p, k],
                    (((1,), (1,)), ((), ())), preferred_element_type=jnp.float32,
                )
            total = total * factor
            psi = jnp.where(farthest < size, block_of(first + k), 0).astype(jnp.float32)
            own_buf[k] = psi
            correlation += jnp.sum(psi * total, keepdims=True)
            norm += jnp.sum(psi * psi, keepdims=True)
            cut = total.reshape(block // rows, rows, block).astype(jnp.bfloat16)
            for part in range(block // LANES):
                at = (part * here + k) * rows
                out_ref[:, at : at + rows, :] = cut[:, :, part * LANES : (part + 1) * LANES]
            own_ref[k] = own_buf[k, pl.ds(start, rows)]
            live_ref[k] = jnp.where(part_farthest < size, 1.0, 0.0)
        high = correlation.astype(jnp.bfloat16).astype(jnp.float32)
        middle = (correlation - high).astype(jnp.bfloat16).astype(jnp.float32)
        low = correlation - high - middle
        lane = lax.broadcasted_iota(jnp.int32, (rows, LANES), 1)
        up = lax.broadcasted_iota(jnp.int32, (rows, LANES), 0)
        words = jnp.where(
            lane == 0, high, jnp.where(lane == 1, middle, jnp.where(lane == 2, low, 0.0))
        )
        words = jnp.where(up == 0, words, 0.0).astype(jnp.bfloat16)
        body_rows = here * rows * (block // LANES)
        out_ref[:, body_rows:, :] = jnp.broadcast_to(words[None], (block // rows, *words.shape))
        norm_ref[...] = jnp.broadcast_to(norm, norm_ref.shape)

    return body


def sum_kernel(received_ref, norm_ref, live_ref, wide_ref, both_ref):
    here, rows, block = wide_ref.shape
    summed = jnp.sum(received_ref[...].astype(jnp.float32), axis=0)
    parts = block // LANES
    correlation = jnp.sum(summed[parts * here * rows :], keepdims=True)
    up = lax.broadcasted_iota(jnp.int32, both_ref.shape[1:], 0)
    both = jnp.where(up == 0, correlation, norm_ref[...])
    both_ref[...] = jnp.broadcast_to(both[None], both_ref.shape)
    for k in range(here):
        for part in range(parts):
            at, lanes = (part * here + k) * rows, slice(part * LANES, (part + 1) * LANES)
            kept = jnp.where(live_ref[k, :, lanes] > 0, summed[at : at + rows], 0.0)
            wide_ref[k, :, lanes] = kept


def residual_kernel(both_ref, wide_ref, own_ref, sigma_ref, out_ref):
    both = jnp.sum(both_ref[...], axis=0)
    ritz_value = both[0:1, 0:1] / both[1:2, 0:1]
    sigma_ref[...] = wide_ref[...].astype(jnp.bfloat16)
    for k in range(wide_ref.shape[0]):
        out_ref[k] = (wide_ref[k] - ritz_value * own_ref[k]).astype(jnp.bfloat16)


def local(wavefunction, left_ops, right_ops, charge, block_sizes):
    here, block, _ = wavefunction.shape
    pairs = left_ops.shape[0]
    ops_count = lax.axis_size("ops")
    sec_total = lax.axis_size("sec")
    sectors = block_sizes.shape[0]
    rows = block // ops_count
    quarter = block // COLOURS
    eighth = quarter // 2
    factor = float(pairs * ops_count) ** (-0.5)
    y_size = ops_count // X_SIZE
    colour = colour_of(lax.axis_index("ops"))
    smem = pl.BlockSpec(memory_space=pltpu.SMEM)
    vmem = pl.BlockSpec(memory_space=pltpu.VMEM)
    bf16, f32 = jnp.bfloat16, jnp.float32

    core = lax.axis_index("sec") % 2
    own = lax.dynamic_slice_in_dim(wavefunction, colour * quarter, quarter, 1)
    halves = own.reshape(here, 2, eighth, block).transpose(1, 0, 2, 3)
    spread = jnp.broadcast_to(halves[None], (sec_total // 2, *halves.shape))
    spread = spread.reshape(sec_total, here, eighth, block)
    own = lax.all_to_all(spread, "sec", 0, 0).reshape(sectors, eighth, block)

    def device(x, y, s):
        return ((y % y_size) * X_SIZE + x % X_SIZE) * sec_total + s

    def fetch(step_x, step_y):
        pairs = []
        for y in range(y_size):
            for x in range(X_SIZE):
                for s in range(sec_total):
                    way = 1 - 2 * (s % 2)
                    pairs.append((device(x + way * step_x, y + way * step_y, s), device(x, y, s)))
        return lax.ppermute(own, ("ops", "sec"), pairs)

    swap = [(s, s ^ 1) for s in range(sec_total)]
    mine = jnp.zeros((sectors, COLOURS, eighth, block), bf16)
    other = mine
    pieces = ((own, 0, 0), (fetch(0, 1), 1, 2), (fetch(1, 0), 2, 0), (fetch(0, -1), 3, -2))
    for piece, relative, way in pieces:
        where = (0, lax.rem(colour + relative + way * core, COLOURS), 0, 0)
        mine = lax.dynamic_update_slice(mine, piece[:, None], where)
        where = (0, lax.rem(colour + relative + way * (1 - core), COLOURS), 0, 0)
        other = lax.dynamic_update_slice(other, lax.ppermute(piece, "sec", swap)[:, None], where)

    part = (here, rows, block)
    pack_rows = here * rows * (block // LANES) + rows
    pieces, norm, own_rows, live = pl.pallas_call(
        sigma_kernel(sectors, rows, factor),
        out_shape=(
            jax.ShapeDtypeStruct((ops_count, pack_rows, LANES), bf16),
            jax.ShapeDtypeStruct((SUBLANES, LANES), f32),
            jax.ShapeDtypeStruct(part, f32),
            jax.ShapeDtypeStruct(part, f32),
        ),
        in_specs=[smem] * 2 + [vmem] * 4,
        out_specs=(vmem,) * 4,
        scratch_shapes=[
            pltpu.VMEM((here, block, pairs * block), bf16),
            pltpu.VMEM((here, block, block), f32),
        ],
        compiler_params=pltpu.CompilerParams(vmem_limit_bytes=VMEM_LIMIT),
        cost_estimate=pl.CostEstimate(
            flops=4 * pairs * here * block**3, bytes_accessed=2**20, transcendentals=0
        ),
    )(charge, block_sizes, mine, other, left_ops, right_ops)
    received = lax.all_to_all(pieces, "ops", 0, 0)

    wide, both = pl.pallas_call(
        sum_kernel,
        out_shape=(
            jax.ShapeDtypeStruct(part, f32),
            jax.ShapeDtypeStruct((sec_total, SUBLANES, LANES), f32),
        ),
        in_specs=[vmem] * 3,
        out_specs=(vmem,) * 2,
        compiler_params=SMALL,
    )(received, norm, live)
    both = lax.all_to_all(both, "sec", 0, 0)
    return pl.pallas_call(
        residual_kernel,
        out_shape=(jax.ShapeDtypeStruct(part, bf16),) * 2,
        in_specs=[vmem] * 3,
        out_specs=(vmem,) * 2,
        compiler_params=SMALL,
    )(both, wide, own_rows)


def solution(mesh):
    placed = (
        P("sec", None, None),
        P("ops", "sec", None, None),
        P("ops", "sec", None, None),
        P("ops"),
        P(),
    )
    return jax.shard_map(
        local,
        mesh=mesh,
        in_specs=placed,
        out_specs=(P("sec", "ops", None), P("sec", "ops", None)),
        check_vma=False,
    )
```

```python
import jax
import jax.numpy as jnp
from jax import lax
from jax.experimental import pallas as pl
from jax.experimental.pallas import tpu as pltpu
from jax.sharding import PartitionSpec as P

LANES = 128
SUBLANES = 8
X_SIZE = 4
COLOURS = 4
VMEM_LIMIT = 16 * 2**20
SMALL = pltpu.CompilerParams(vmem_limit_bytes=4 * 2**20)


def colour_of(slot):
    return lax.rem(2 * lax.rem(slot, X_SIZE) + lax.div(slot, X_SIZE), COLOURS)


def left_kernel(sectors, rows):
    def body(
        charge_ref, sizes_ref, mine_ref, other_ref, left_ref,
        half_ref, psi_ref, norm_ref, own_ref, live_ref, own_buf,
    ):
        pairs, here, block, _ = left_ref.shape
        sec = lax.axis_index("sec")
        first = sec * here
        start = pl.multiple_of(lax.axis_index("ops") * rows, rows)
        core = lax.rem(sec, 2)
        lane = lax.broadcasted_iota(jnp.int32, (1, block), 1)

        def block_of(source):
            mine, other = mine_ref[source], other_ref[source]
            upper = jnp.where(core == 0, mine, other)
            lower = jnp.where(core == 0, other, mine)
            eighths = [part[q] for q in range(COLOURS) for part in (upper, lower)]
            return jnp.concatenate(eighths, axis=0)

        for p in range(pairs):
            for k in range(here):
                source = lax.rem(first + k + charge_ref[p], sectors)
                live = jnp.where(lane < sizes_ref[source], 1.0, 0.0)
                left = left_ref[p, k] * live.astype(jnp.bfloat16)
                half = jnp.dot(left, block_of(source), preferred_element_type=jnp.float32) * live
                half_ref[k, :, p * block : (p + 1) * block] = half.astype(jnp.bfloat16)
        row = lax.broadcasted_iota(jnp.int32, (block, block), 0)
        column = lax.broadcasted_iota(jnp.int32, (block, block), 1)
        farthest = jnp.maximum(row, column)
        part_row = lax.broadcasted_iota(jnp.int32, (rows, block), 0) + start
        part_farthest = jnp.maximum(part_row, lax.broadcasted_iota(jnp.int32, (rows, block), 1))
        norm = jnp.zeros((1, 1), jnp.float32)
        for k in range(here):
            size = sizes_ref[first + k]
            psi = jnp.where(farthest < size, block_of(first + k), 0)
            psi_ref[k] = psi
            psi = psi.astype(jnp.float32)
            own_buf[...] = psi
            norm += jnp.sum(psi * psi, keepdims=True)
            own_ref[k] = own_buf[pl.ds(start, rows), :]
            live_ref[k] = jnp.where(part_farthest < size, 1.0, 0.0)
        norm_ref[...] = jnp.broadcast_to(norm, norm_ref.shape)

    return body


def right_kernel(rows, factor):
    def body(half_ref, psi_ref, right_ref, out_ref):
        pairs, here, block, _ = right_ref.shape
        correlation = jnp.zeros((1, 1), jnp.float32)
        for k in range(here):
            total = jnp.zeros((block, block), jnp.float32)
            for p in range(pairs):
                total += lax.dot_general(
                    half_ref[k, :, p * block : (p + 1) * block], right_ref[p, k],
                    (((1,), (1,)), ((), ())), preferred_element_type=jnp.float32,
                )
            total = total * factor
            correlation += jnp.sum(psi_ref[k].astype(jnp.float32) * total, keepdims=True)
            cut = total.reshape(block // rows, rows, block).astype(jnp.bfloat16)
            for part in range(block // LANES):
                at = (part * here + k) * rows
                out_ref[:, at : at + rows, :] = cut[:, :, part * LANES : (part + 1) * LANES]
        high = correlation.astype(jnp.bfloat16).astype(jnp.float32)
        middle = (correlation - high).astype(jnp.bfloat16).astype(jnp.float32)
        low = correlation - high - middle
        lane = lax.broadcasted_iota(jnp.int32, (rows, LANES), 1)
        up = lax.broadcasted_iota(jnp.int32, (rows, LANES), 0)
        words = jnp.where(
            lane == 0, high, jnp.where(lane == 1, middle, jnp.where(lane == 2, low, 0.0))
        )
        words = jnp.where(up == 0, words, 0.0).astype(jnp.bfloat16)
        body_rows = here * rows * (block // LANES)
        out_ref[:, body_rows:, :] = jnp.broadcast_to(words[None], (block // rows, *words.shape))

    return body


def sum_kernel(received_ref, norm_ref, live_ref, wide_ref, both_ref):
    here, rows, block = wide_ref.shape
    summed = jnp.sum(received_ref[...].astype(jnp.float32), axis=0)
    parts = block // LANES
    correlation = jnp.sum(summed[parts * here * rows :], keepdims=True)
    up = lax.broadcasted_iota(jnp.int32, both_ref.shape[1:], 0)
    both = jnp.where(up == 0, correlation, norm_ref[...])
    both_ref[...] = jnp.broadcast_to(both[None], both_ref.shape)
    for k in range(here):
        for part in range(parts):
            at, lanes = (part * here + k) * rows, slice(part * LANES, (part + 1) * LANES)
            kept = jnp.where(live_ref[k, :, lanes] > 0, summed[at : at + rows], 0.0)
            wide_ref[k, :, lanes] = kept


def residual_kernel(both_ref, wide_ref, own_ref, sigma_ref, out_ref):
    both = jnp.sum(both_ref[...], axis=0)
    ritz_value = both[0:1, 0:1] / both[1:2, 0:1]
    sigma_ref[...] = wide_ref[...].astype(jnp.bfloat16)
    for k in range(wide_ref.shape[0]):
        out_ref[k] = (wide_ref[k] - ritz_value * own_ref[k]).astype(jnp.bfloat16)


def local(wavefunction, left_ops, right_ops, charge, block_sizes):
    here, block, _ = wavefunction.shape
    pairs = left_ops.shape[0]
    ops_count = lax.axis_size("ops")
    sec_total = lax.axis_size("sec")
    sectors = block_sizes.shape[0]
    rows = block // ops_count
    quarter = block // COLOURS
    eighth = quarter // 2
    factor = float(pairs * ops_count) ** (-0.5)
    y_size = ops_count // X_SIZE
    colour = colour_of(lax.axis_index("ops"))
    smem = pl.BlockSpec(memory_space=pltpu.SMEM)
    vmem = pl.BlockSpec(memory_space=pltpu.VMEM)
    bf16, f32 = jnp.bfloat16, jnp.float32

    core = lax.axis_index("sec") % 2
    own = lax.dynamic_slice_in_dim(wavefunction, colour * quarter, quarter, 1)
    halves = own.reshape(here, 2, eighth, block).transpose(1, 0, 2, 3)
    spread = jnp.broadcast_to(halves[None], (sec_total // 2, *halves.shape))
    spread = spread.reshape(sec_total, here, eighth, block)
    own = lax.all_to_all(spread, "sec", 0, 0).reshape(sectors, eighth, block)

    def device(x, y, s):
        return ((y % y_size) * X_SIZE + x % X_SIZE) * sec_total + s

    def fetch(step_x, step_y):
        pairs = []
        for y in range(y_size):
            for x in range(X_SIZE):
                for s in range(sec_total):
                    way = 1 - 2 * (s % 2)
                    pairs.append((device(x + way * step_x, y + way * step_y, s), device(x, y, s)))
        return lax.ppermute(own, ("ops", "sec"), pairs)

    swap = [(s, s ^ 1) for s in range(sec_total)]
    mine = jnp.zeros((sectors, COLOURS, eighth, block), bf16)
    other = mine
    pieces = ((own, 0, 0), (fetch(0, 1), 1, 2), (fetch(1, 0), 2, 0), (fetch(0, -1), 3, -2))
    for piece, relative, way in pieces:
        where = (0, lax.rem(colour + relative + way * core, COLOURS), 0, 0)
        mine = lax.dynamic_update_slice(mine, piece[:, None], where)
        where = (0, lax.rem(colour + relative + way * (1 - core), COLOURS), 0, 0)
        other = lax.dynamic_update_slice(other, lax.ppermute(piece, "sec", swap)[:, None], where)

    part = (here, rows, block)
    pack_rows = here * rows * (block // LANES) + rows
    half, psi, norm, own_rows, live = pl.pallas_call(
        left_kernel(sectors, rows),
        out_shape=(
            jax.ShapeDtypeStruct((here, block, pairs * block), bf16),
            jax.ShapeDtypeStruct(wavefunction.shape, bf16),
            jax.ShapeDtypeStruct((SUBLANES, LANES), f32),
            jax.ShapeDtypeStruct(part, f32),
            jax.ShapeDtypeStruct(part, f32),
        ),
        in_specs=[smem] * 2 + [vmem] * 3,
        out_specs=(vmem,) * 5,
        scratch_shapes=[pltpu.VMEM((block, block), f32)],
        compiler_params=pltpu.CompilerParams(vmem_limit_bytes=VMEM_LIMIT),
        cost_estimate=pl.CostEstimate(
            flops=2 * pairs * here * block**3, bytes_accessed=2**20, transcendentals=0
        ),
    )(charge, block_sizes, mine, other, left_ops)
    pieces = pl.pallas_call(
        right_kernel(rows, factor),
        out_shape=jax.ShapeDtypeStruct((ops_count, pack_rows, LANES), bf16),
        in_specs=[vmem] * 3,
        out_specs=vmem,
        compiler_params=pltpu.CompilerParams(vmem_limit_bytes=VMEM_LIMIT),
        cost_estimate=pl.CostEstimate(
            flops=2 * pairs * here * block**3, bytes_accessed=2**20, transcendentals=0
        ),
    )(half, psi, right_ops)
    received = lax.all_to_all(pieces, "ops", 0, 0)

    wide, both = pl.pallas_call(
        sum_kernel,
        out_shape=(
            jax.ShapeDtypeStruct(part, f32),
            jax.ShapeDtypeStruct((sec_total, SUBLANES, LANES), f32),
        ),
        in_specs=[vmem] * 3,
        out_specs=(vmem,) * 2,
        compiler_params=SMALL,
    )(received, norm, live)
    both = lax.all_to_all(both, "sec", 0, 0)
    return pl.pallas_call(
        residual_kernel,
        out_shape=(jax.ShapeDtypeStruct(part, bf16),) * 2,
        in_specs=[vmem] * 3,
        out_specs=(vmem,) * 2,
        compiler_params=SMALL,
    )(both, wide, own_rows)


def solution(mesh):
    placed = (
        P("sec", None, None),
        P("ops", "sec", None, None),
        P("ops", "sec", None, None),
        P("ops"),
        P(),
    )
    return jax.shard_map(
        local,
        mesh=mesh,
        in_specs=placed,
        out_specs=(P("sec", "ops", None), P("sec", "ops", None)),
        check_vma=False,
    )
```

```python
import jax
import jax.numpy as jnp
from jax import lax
from jax.experimental import pallas as pl
from jax.experimental.pallas import tpu as pltpu
from jax.sharding import PartitionSpec as P

LANES = 128
SUBLANES = 8
X_SIZE = 4
COLOURS = 4
VMEM_LIMIT = 16 * 2**20
SMALL = pltpu.CompilerParams(vmem_limit_bytes=4 * 2**20)


def colour_of(slot):
    return lax.rem(2 * lax.rem(slot, X_SIZE) + lax.div(slot, X_SIZE), COLOURS)


def left_kernel(sectors, rows):
    def body(
        charge_ref, sizes_ref, mine_ref, other_ref, left_ref,
        half_ref, psi_ref, norm_ref, own_ref, live_ref, own_buf,
    ):
        pairs, here, block, _ = left_ref.shape
        sec = lax.axis_index("sec")
        first = sec * here
        start = pl.multiple_of(lax.axis_index("ops") * rows, rows)
        core = lax.rem(sec, 2)
        lane = lax.broadcasted_iota(jnp.int32, (1, block), 1)

        def block_of(source):
            mine, other = mine_ref[source], other_ref[source]
            upper = jnp.where(core == 0, mine, other)
            lower = jnp.where(core == 0, other, mine)
            eighths = [part[q] for q in range(COLOURS) for part in (upper, lower)]
            return jnp.concatenate(eighths, axis=0)

        for p in range(pairs):
            for k in range(here):
                source = lax.rem(first + k + charge_ref[p], sectors)
                live = jnp.where(lane < sizes_ref[source], 1.0, 0.0)
                left = left_ref[p, k] * live.astype(jnp.bfloat16)
                half = jnp.dot(left, block_of(source), preferred_element_type=jnp.float32) * live
                half_ref[k, :, p * block : (p + 1) * block] = half.astype(jnp.bfloat16)
        row = lax.broadcasted_iota(jnp.int32, (block, block), 0)
        column = lax.broadcasted_iota(jnp.int32, (block, block), 1)
        farthest = jnp.maximum(row, column)
        part_row = lax.broadcasted_iota(jnp.int32, (rows, block), 0) + start
        part_farthest = jnp.maximum(part_row, lax.broadcasted_iota(jnp.int32, (rows, block), 1))
        norm = jnp.zeros((1, 1), jnp.float32)
        for k in range(here):
            size = sizes_ref[first + k]
            psi = jnp.where(farthest < size, block_of(first + k), 0)
            psi_ref[k] = psi
            psi = psi.astype(jnp.float32)
            own_buf[...] = psi
            norm += jnp.sum(psi * psi, keepdims=True)
            own_ref[k] = own_buf[pl.ds(start, rows), :]
            live_ref[k] = jnp.where(part_farthest < size, 1.0, 0.0)
        norm_ref[...] = jnp.broadcast_to(norm, norm_ref.shape)

    return body


def right_kernel(rows, factor):
    def body(half_ref, psi_ref, right_ref, out_ref):
        pairs, here, block, _ = right_ref.shape
        correlation = jnp.zeros((1, 1), jnp.float32)
        for k in range(here):
            total = jnp.zeros((block, block), jnp.float32)
            for p in range(pairs):
                total += lax.dot_general(
                    half_ref[k, :, p * block : (p + 1) * block], right_ref[p, k],
                    (((1,), (1,)), ((), ())), preferred_element_type=jnp.float32,
                )
            total = total * factor
            correlation += jnp.sum(psi_ref[k].astype(jnp.float32) * total, keepdims=True)
            cut = total.reshape(block // rows, rows, block).astype(jnp.bfloat16)
            for part in range(block // LANES):
                at = (part * here + k) * rows
                out_ref[:, at : at + rows, :] = cut[:, :, part * LANES : (part + 1) * LANES]
        high = correlation.astype(jnp.bfloat16).astype(jnp.float32)
        middle = (correlation - high).astype(jnp.bfloat16).astype(jnp.float32)
        low = correlation - high - middle
        lane = lax.broadcasted_iota(jnp.int32, (rows, LANES), 1)
        up = lax.broadcasted_iota(jnp.int32, (rows, LANES), 0)
        words = jnp.where(
            lane == 0, high, jnp.where(lane == 1, middle, jnp.where(lane == 2, low, 0.0))
        )
        words = jnp.where(up == 0, words, 0.0).astype(jnp.bfloat16)
        body_rows = here * rows * (block // LANES)
        out_ref[:, body_rows:, :] = jnp.broadcast_to(words[None], (block // rows, *words.shape))

    return body


def sum_kernel(received_ref, norm_ref, live_ref, wide_ref, both_ref):
    here, rows, block = wide_ref.shape
    summed = jnp.sum(received_ref[...].astype(jnp.float32), axis=0)
    parts = block // LANES
    correlation = jnp.sum(summed[parts * here * rows :], keepdims=True)
    lane = lax.broadcasted_iota(jnp.int32, (1, LANES), 1)
    both = jnp.where(lane == 0, correlation, norm_ref[0:1, :])
    both_ref[...] = jnp.broadcast_to(both[None], both_ref.shape)
    for k in range(here):
        for part in range(parts):
            at, lanes = (part * here + k) * rows, slice(part * LANES, (part + 1) * LANES)
            kept = jnp.where(live_ref[k, :, lanes] > 0, summed[at : at + rows], 0.0)
            wide_ref[k, :, lanes] = kept


def residual_kernel(both_ref, wide_ref, own_ref, sigma_ref, out_ref):
    both = jnp.sum(both_ref[...], axis=0)
    ritz_value = both[0:1, 0:1] / both[0:1, 1:2]
    sigma_ref[...] = wide_ref[...].astype(jnp.bfloat16)
    for k in range(wide_ref.shape[0]):
        out_ref[k] = (wide_ref[k] - ritz_value * own_ref[k]).astype(jnp.bfloat16)


def local(wavefunction, left_ops, right_ops, charge, block_sizes):
    here, block, _ = wavefunction.shape
    pairs = left_ops.shape[0]
    ops_count = lax.axis_size("ops")
    sec_total = lax.axis_size("sec")
    sectors = block_sizes.shape[0]
    rows = block // ops_count
    quarter = block // COLOURS
    eighth = quarter // 2
    factor = float(pairs * ops_count) ** (-0.5)
    y_size = ops_count // X_SIZE
    colour = colour_of(lax.axis_index("ops"))
    smem = pl.BlockSpec(memory_space=pltpu.SMEM)
    vmem = pl.BlockSpec(memory_space=pltpu.VMEM)
    bf16, f32 = jnp.bfloat16, jnp.float32

    core = lax.axis_index("sec") % 2
    own = lax.dynamic_slice_in_dim(wavefunction, colour * quarter, quarter, 1)
    halves = own.reshape(here, 2, eighth, block).transpose(1, 0, 2, 3)
    spread = jnp.broadcast_to(halves[None], (sec_total // 2, *halves.shape))
    spread = spread.reshape(sec_total, here, eighth, block)
    own = lax.all_to_all(spread, "sec", 0, 0).reshape(sectors, eighth, block)

    def device(x, y, s):
        return ((y % y_size) * X_SIZE + x % X_SIZE) * sec_total + s

    def fetch(step_x, step_y):
        pairs = []
        for y in range(y_size):
            for x in range(X_SIZE):
                for s in range(sec_total):
                    way = 1 - 2 * (s % 2)
                    pairs.append((device(x + way * step_x, y + way * step_y, s), device(x, y, s)))
        return lax.ppermute(own, ("ops", "sec"), pairs)

    swap = [(s, s ^ 1) for s in range(sec_total)]
    mine = jnp.zeros((sectors, COLOURS, eighth, block), bf16)
    other = mine
    pieces = ((own, 0, 0), (fetch(0, 1), 1, 2), (fetch(1, 0), 2, 0), (fetch(0, -1), 3, -2))
    for piece, relative, way in pieces:
        where = (0, lax.rem(colour + relative + way * core, COLOURS), 0, 0)
        mine = lax.dynamic_update_slice(mine, piece[:, None], where)
        where = (0, lax.rem(colour + relative + way * (1 - core), COLOURS), 0, 0)
        other = lax.dynamic_update_slice(other, lax.ppermute(piece, "sec", swap)[:, None], where)

    part = (here, rows, block)
    pack_rows = here * rows * (block // LANES) + rows
    half, psi, norm, own_rows, live = pl.pallas_call(
        left_kernel(sectors, rows),
        out_shape=(
            jax.ShapeDtypeStruct((here, block, pairs * block), bf16),
            jax.ShapeDtypeStruct(wavefunction.shape, bf16),
            jax.ShapeDtypeStruct((SUBLANES, LANES), f32),
            jax.ShapeDtypeStruct(part, f32),
            jax.ShapeDtypeStruct(part, f32),
        ),
        in_specs=[smem] * 2 + [vmem] * 3,
        out_specs=(vmem,) * 5,
        scratch_shapes=[pltpu.VMEM((block, block), f32)],
        compiler_params=pltpu.CompilerParams(vmem_limit_bytes=VMEM_LIMIT),
        cost_estimate=pl.CostEstimate(
            flops=2 * pairs * here * block**3, bytes_accessed=2**20, transcendentals=0
        ),
    )(charge, block_sizes, mine, other, left_ops)
    pieces = pl.pallas_call(
        right_kernel(rows, factor),
        out_shape=jax.ShapeDtypeStruct((ops_count, pack_rows, LANES), bf16),
        in_specs=[vmem] * 3,
        out_specs=vmem,
        compiler_params=pltpu.CompilerParams(vmem_limit_bytes=VMEM_LIMIT),
        cost_estimate=pl.CostEstimate(
            flops=2 * pairs * here * block**3, bytes_accessed=2**20, transcendentals=0
        ),
    )(half, psi, right_ops)
    received = lax.all_to_all(pieces, "ops", 0, 0)

    wide, both = pl.pallas_call(
        sum_kernel,
        out_shape=(
            jax.ShapeDtypeStruct(part, f32),
            jax.ShapeDtypeStruct((sec_total, 1, LANES), f32),
        ),
        in_specs=[vmem] * 3,
        out_specs=(vmem,) * 2,
        compiler_params=SMALL,
    )(received, norm, live)
    both = lax.all_to_all(both, "sec", 0, 0)
    return pl.pallas_call(
        residual_kernel,
        out_shape=(jax.ShapeDtypeStruct(part, bf16),) * 2,
        in_specs=[vmem] * 3,
        out_specs=(vmem,) * 2,
        compiler_params=SMALL,
    )(both, wide, own_rows)


def solution(mesh):
    placed = (
        P("sec", None, None),
        P("ops", "sec", None, None),
        P("ops", "sec", None, None),
        P("ops"),
        P(),
    )
    return jax.shard_map(
        local,
        mesh=mesh,
        in_specs=placed,
        out_specs=(P("sec", "ops", None), P("sec", "ops", None)),
        check_vma=False,
    )
```

```python
import jax
import jax.numpy as jnp
from jax import lax
from jax.experimental import pallas as pl
from jax.experimental.pallas import tpu as pltpu
from jax.sharding import PartitionSpec as P

LANES = 128
SUBLANES = 8
X_SIZE = 4
COLOURS = 4
VMEM_LIMIT = 16 * 2**20
SMALL = pltpu.CompilerParams(vmem_limit_bytes=4 * 2**20)


def colour_of(slot):
    return lax.rem(2 * lax.rem(slot, X_SIZE) + lax.div(slot, X_SIZE), COLOURS)


def left_kernel(sectors, rows):
    def body(
        charge_ref, sizes_ref, all_ref, left_ref,
        half_ref, psi_ref, norm_ref, own_ref, live_ref, own_buf,
    ):
        pairs, here, block, _ = left_ref.shape
        sec = lax.axis_index("sec")
        first = sec * here
        start = pl.multiple_of(lax.axis_index("ops") * rows, rows)
        lane = lax.broadcasted_iota(jnp.int32, (1, block), 1)

        for p in range(pairs):
            for k in range(here):
                source = lax.rem(first + k + charge_ref[p], sectors)
                live = jnp.where(lane < sizes_ref[source], 1.0, 0.0)
                left = left_ref[p, k] * live.astype(jnp.bfloat16)
                half = jnp.dot(left, all_ref[source], preferred_element_type=jnp.float32) * live
                half_ref[k, :, p * block : (p + 1) * block] = half.astype(jnp.bfloat16)
        row = lax.broadcasted_iota(jnp.int32, (block, block), 0)
        column = lax.broadcasted_iota(jnp.int32, (block, block), 1)
        farthest = jnp.maximum(row, column)
        part_row = lax.broadcasted_iota(jnp.int32, (rows, block), 0) + start
        part_farthest = jnp.maximum(part_row, lax.broadcasted_iota(jnp.int32, (rows, block), 1))
        norm = jnp.zeros((1, 1), jnp.float32)
        for k in range(here):
            size = sizes_ref[first + k]
            psi = jnp.where(farthest < size, all_ref[first + k], 0)
            psi_ref[k] = psi
            psi = psi.astype(jnp.float32)
            own_buf[...] = psi
            norm += jnp.sum(psi * psi, keepdims=True)
            own_ref[k] = own_buf[pl.ds(start, rows), :]
            live_ref[k] = jnp.where(part_farthest < size, 1.0, 0.0)
        norm_ref[...] = jnp.broadcast_to(norm, norm_ref.shape)

    return body


def right_kernel(rows, factor):
    def body(half_ref, psi_ref, right_ref, out_ref):
        pairs, here, block, _ = right_ref.shape
        correlation = jnp.zeros((1, 1), jnp.float32)
        for k in range(here):
            total = jnp.zeros((block, block), jnp.float32)
            for p in range(pairs):
                total += lax.dot_general(
                    half_ref[k, :, p * block : (p + 1) * block], right_ref[p, k],
                    (((1,), (1,)), ((), ())), preferred_element_type=jnp.float32,
                )
            total = total * factor
            correlation += jnp.sum(psi_ref[k].astype(jnp.float32) * total, keepdims=True)
            cut = total.reshape(block // rows, rows, block).astype(jnp.bfloat16)
            for part in range(block // LANES):
                at = (part * here + k) * rows
                out_ref[:, at : at + rows, :] = cut[:, :, part * LANES : (part + 1) * LANES]
        high = correlation.astype(jnp.bfloat16).astype(jnp.float32)
        middle = (correlation - high).astype(jnp.bfloat16).astype(jnp.float32)
        low = correlation - high - middle
        lane = lax.broadcasted_iota(jnp.int32, (rows, LANES), 1)
        up = lax.broadcasted_iota(jnp.int32, (rows, LANES), 0)
        words = jnp.where(
            lane == 0, high, jnp.where(lane == 1, middle, jnp.where(lane == 2, low, 0.0))
        )
        words = jnp.where(up == 0, words, 0.0).astype(jnp.bfloat16)
        body_rows = here * rows * (block // LANES)
        out_ref[:, body_rows:, :] = jnp.broadcast_to(words[None], (block // rows, *words.shape))

    return body


def sum_kernel(received_ref, norm_ref, live_ref, wide_ref, both_ref):
    here, rows, block = wide_ref.shape
    summed = jnp.sum(received_ref[...].astype(jnp.float32), axis=0)
    parts = block // LANES
    correlation = jnp.sum(summed[parts * here * rows :], keepdims=True)
    lane = lax.broadcasted_iota(jnp.int32, (1, LANES), 1)
    both = jnp.where(lane == 0, correlation, norm_ref[0:1, :])
    both_ref[...] = jnp.broadcast_to(both[None], both_ref.shape)
    for k in range(here):
        for part in range(parts):
            at, lanes = (part * here + k) * rows, slice(part * LANES, (part + 1) * LANES)
            kept = jnp.where(live_ref[k, :, lanes] > 0, summed[at : at + rows], 0.0)
            wide_ref[k, :, lanes] = kept


def residual_kernel(both_ref, wide_ref, own_ref, sigma_ref, out_ref):
    both = jnp.sum(both_ref[...], axis=0)
    ritz_value = both[0:1, 0:1] / both[0:1, 1:2]
    sigma_ref[...] = wide_ref[...].astype(jnp.bfloat16)
    for k in range(wide_ref.shape[0]):
        out_ref[k] = (wide_ref[k] - ritz_value * own_ref[k]).astype(jnp.bfloat16)


def local(wavefunction, left_ops, right_ops, charge, block_sizes):
    here, block, _ = wavefunction.shape
    pairs = left_ops.shape[0]
    ops_count = lax.axis_size("ops")
    sec_total = lax.axis_size("sec")
    sectors = block_sizes.shape[0]
    rows = block // ops_count
    quarter = block // COLOURS
    eighth = quarter // 2
    factor = float(pairs * ops_count) ** (-0.5)
    y_size = ops_count // X_SIZE
    colour = colour_of(lax.axis_index("ops"))
    smem = pl.BlockSpec(memory_space=pltpu.SMEM)
    vmem = pl.BlockSpec(memory_space=pltpu.VMEM)
    bf16, f32 = jnp.bfloat16, jnp.float32

    core = lax.axis_index("sec") % 2
    own = lax.dynamic_slice_in_dim(wavefunction, colour * quarter, quarter, 1)
    halves = own.reshape(here, 2, eighth, block).transpose(1, 0, 2, 3)
    spread = jnp.broadcast_to(halves[None], (sec_total // 2, *halves.shape))
    spread = spread.reshape(sec_total, here, eighth, block)
    own = lax.all_to_all(spread, "sec", 0, 0).reshape(sectors, eighth, block)

    def device(x, y, s):
        return ((y % y_size) * X_SIZE + x % X_SIZE) * sec_total + s

    def fetch(step_x, step_y):
        pairs = []
        for y in range(y_size):
            for x in range(X_SIZE):
                for s in range(sec_total):
                    way = 1 - 2 * (s % 2)
                    pairs.append((device(x + way * step_x, y + way * step_y, s), device(x, y, s)))
        return lax.ppermute(own, ("ops", "sec"), pairs)

    swap = [(s, s ^ 1) for s in range(sec_total)]
    everything = jnp.zeros((sectors, COLOURS, 2, eighth, block), bf16)
    pieces = ((own, 0, 0), (fetch(0, 1), 1, 2), (fetch(1, 0), 2, 0), (fetch(0, -1), 3, -2))
    for piece, relative, way in pieces:
        for part, side in ((piece, core), (lax.ppermute(piece, "sec", swap), 1 - core)):
            where = (0, lax.rem(colour + relative + way * side, COLOURS), side, 0, 0)
            everything = lax.dynamic_update_slice(everything, part[:, None, None], where)
    everything = everything.reshape(sectors, block, block)

    part = (here, rows, block)
    pack_rows = here * rows * (block // LANES) + rows
    half, psi, norm, own_rows, live = pl.pallas_call(
        left_kernel(sectors, rows),
        out_shape=(
            jax.ShapeDtypeStruct((here, block, pairs * block), bf16),
            jax.ShapeDtypeStruct(wavefunction.shape, bf16),
            jax.ShapeDtypeStruct((SUBLANES, LANES), f32),
            jax.ShapeDtypeStruct(part, f32),
            jax.ShapeDtypeStruct(part, f32),
        ),
        in_specs=[smem] * 2 + [vmem] * 2,
        out_specs=(vmem,) * 5,
        scratch_shapes=[pltpu.VMEM((block, block), f32)],
        compiler_params=pltpu.CompilerParams(vmem_limit_bytes=VMEM_LIMIT),
        cost_estimate=pl.CostEstimate(
            flops=2 * pairs * here * block**3, bytes_accessed=2**20, transcendentals=0
        ),
    )(charge, block_sizes, everything, left_ops)
    pieces = pl.pallas_call(
        right_kernel(rows, factor),
        out_shape=jax.ShapeDtypeStruct((ops_count, pack_rows, LANES), bf16),
        in_specs=[vmem] * 3,
        out_specs=vmem,
        compiler_params=pltpu.CompilerParams(vmem_limit_bytes=VMEM_LIMIT),
        cost_estimate=pl.CostEstimate(
            flops=2 * pairs * here * block**3, bytes_accessed=2**20, transcendentals=0
        ),
    )(half, psi, right_ops)
    received = lax.all_to_all(pieces, "ops", 0, 0)

    wide, both = pl.pallas_call(
        sum_kernel,
        out_shape=(
            jax.ShapeDtypeStruct(part, f32),
            jax.ShapeDtypeStruct((sec_total, 1, LANES), f32),
        ),
        in_specs=[vmem] * 3,
        out_specs=(vmem,) * 2,
        compiler_params=SMALL,
    )(received, norm, live)
    both = lax.all_to_all(both, "sec", 0, 0)
    return pl.pallas_call(
        residual_kernel,
        out_shape=(jax.ShapeDtypeStruct(part, bf16),) * 2,
        in_specs=[vmem] * 3,
        out_specs=(vmem,) * 2,
        compiler_params=SMALL,
    )(both, wide, own_rows)


def solution(mesh):
    placed = (
        P("sec", None, None),
        P("ops", "sec", None, None),
        P("ops", "sec", None, None),
        P("ops"),
        P(),
    )
    return jax.shard_map(
        local,
        mesh=mesh,
        in_specs=placed,
        out_specs=(P("sec", "ops", None), P("sec", "ops", None)),
        check_vma=False,
    )
```
